32 devices in a mesh: rows: 4 (over y, core), acts: 8 (over z, x).
Axes of the slice: x: 2, y: 2, z: 4, core: 2. Of those that a mesh axis runs over, the one named last changes fastest.
Arguments:
- features: bfloat16 [16384, 2048], P('rows'), may hold values from -6 to 80
- policy_weight: bfloat16 [2048, 4096], P(None, 'acts'), may hold values from -3 to 3
- reward_weight: bfloat16 [2048, 4096], P(None, 'acts'), may hold values from -1 to 1
- logged_action: int32 [16384], P('rows'), may hold values from 0 to 4095
- reward_level: int32 [16384], P('rows'), may hold values from 0 to 4
- logged_propensity: float32 [16384], P('rows'), may hold values from 9.765625e-05 to 0.0009765625
Outputs:
- policy_grad: float32 [2048, 4096], P(None, 'acts')
- reward_grad: float32 [2048, 4096], P(None, 'acts')
- row_value: float32 [16384], P('rows')
The draws below stay inside these ranges and needn't reach their ends.
All inputs are finite; a program needn't handle non-finite values.
Results may differ from the reference program's by a relative error of at most 0.015.
Values may be sent and summed in bfloat16 or wider, within the bound.
A program may use at most 128 MiB of HBM per device.

```python
import math
import jax
import jax.numpy as jnp
import numpy as np
from jax import lax

D = 2048
ACTIONS = 4096
ROW_DEV = 4096
ROWS = 16384
N_ROWS = 4


def draw_features(key, part):
    own_key = jax.random.fold_in(key, 21)
    values = jnp.clip(jax.random.normal(own_key, (ROWS, D), jnp.float32), -6.0, 6.0)
    return values.astype(jnp.bfloat16)


def draw_policy_weight(key, part):
    own_key = jax.random.fold_in(key, 31)
    values = jnp.clip(jax.random.normal(own_key, (D, ACTIONS), jnp.float32), -6.0, 6.0) / jnp.sqrt(jnp.float32(D))
    return values.astype(jnp.bfloat16)


def draw_reward_weight(key, part):
    own_key = jax.random.fold_in(key, 41)
    scale = 1.0 / jnp.sqrt(jnp.float32(D))
    values = jnp.clip(jax.random.normal(own_key, (D, ACTIONS), jnp.float32), -6.0, 6.0) * scale
    shared = jnp.clip(jax.random.normal(jax.random.fold_in(key, 5), (D,), jnp.float32), -6.0, 6.0) * scale
    return jnp.clip(values + shared[:, None], -1.0, 1.0).astype(jnp.bfloat16)


def plant(values, rng, smallest, high):
    shape = values.shape
    place = [jax.random.randint(jax.random.fold_in(rng, axis), (), 0, shape[axis]) for axis in range(len(shape))]
    values = values.at[tuple(place)].set(smallest)
    longest = shape.index(max(shape))
    place[longest] = (place[longest] + 1) % shape[longest]
    return values.at[tuple(place)].set(high)


def level_of(key, dims, shards, least, top_value):
    loudness, own = 1.0, jax.random.fold_in(key, 6)
    for position, shards_of in shards:
        draws = jnp.exp(jax.random.uniform(jax.random.fold_in(own, position), (shards_of,), jnp.float32, least / len(shards), top_value / len(shards)))
        loudness = loudness * jnp.repeat(draws, dims[position] // shards_of).reshape([-1 if axis == position else 1 for axis in range(len(dims))])
    return loudness


def cumulative_ranks(amount, skew):
    loads = [(1 << 20) // math.isqrt(standing ** skew) + 1 for standing in range(1, amount + 1)]
    width = 1 + sum(loads) // (1 << 30)
    return np.cumsum(np.array([max(1, weight // width) for weight in loads]))


def skewed_ids(key, extent, amount, skew):
    grid = cumulative_ranks(amount, skew)
    pick = jax.random.randint(jax.random.fold_in(key, 1), extent, 0, int(grid[amount - 1]))
    standing = jnp.searchsorted(jnp.asarray(grid, jnp.int32), pick, side="right")
    return jax.random.permutation(jax.random.fold_in(key, 2), amount)[standing].astype(jnp.int32)


def setup_inputs(seed: int = 0) -> dict:
    arg_keys = jax.random.split(jax.random.key(seed), 7)
    features = draw_features(jax.random.fold_in(arg_keys[6], 71), 0)
    policy_weight = draw_policy_weight(jax.random.fold_in(arg_keys[6], 71), 0)
    reward_weight = draw_reward_weight(jax.random.fold_in(arg_keys[6], 71), 0)
    logged_action = plant(skewed_ids(arg_keys[3], (ROWS,), ACTIONS, 2), jax.random.fold_in(arg_keys[3], 3), 0, ACTIONS - 1).astype(jnp.int32)
    reward_level = plant(jax.random.randint(arg_keys[4], (ROWS,), 0, 5), jax.random.fold_in(arg_keys[4], 1), 0, 4).astype(jnp.int32)
    logged_propensity = jnp.clip(jnp.exp(math.log(0.0009765625) - 2.3025851 * jax.random.uniform(arg_keys[5], (ROWS,), jnp.float32) ** level_of(arg_keys[5], (ROWS,), ((0, 4),), -0.2, 0.2)), 9.765625145519152e-05, 0.0009765625)
    return dict(features=features, policy_weight=policy_weight, reward_weight=reward_weight, logged_action=logged_action, reward_level=reward_level, logged_propensity=logged_propensity)


def reference(features, policy_weight, reward_weight, logged_action, reward_level, logged_propensity):
    scores = jnp.dot(features, policy_weight, preferred_element_type=jnp.float32)
    predicted = jnp.dot(features, reward_weight, preferred_element_type=jnp.float32)
    largest = jnp.max(scores, axis=1, keepdims=True)
    exponent = jnp.exp(scores - largest)
    row_total = jnp.sum(exponent, axis=1)
    weighted = jnp.sum(exponent * predicted, axis=1)
    columns = jnp.arange(ACTIONS, dtype=jnp.int32)
    onehot = logged_action[:, None] == columns[None, :]
    picked_exp = jnp.sum(jnp.where(onehot, exponent, jnp.float32(0.0)), axis=1)
    picked_pred = jnp.sum(jnp.where(onehot, predicted, jnp.float32(0.0)), axis=1)
    payoff = reward_level.astype(jnp.float32) * 0.25
    probability = exponent / row_total[:, None]
    mean_pred = weighted / row_total
    importance = picked_exp / row_total / logged_propensity
    corrected = importance * (payoff - picked_pred)
    row_value = mean_pred + corrected
    policy_term = (probability * (predicted - mean_pred[:, None])
                   + corrected[:, None] * (onehot.astype(jnp.float32) - probability)).astype(jnp.bfloat16)
    reward_term = jnp.where(onehot, predicted - payoff[:, None], jnp.float32(0.0)).astype(jnp.bfloat16)
    both_terms = jnp.concatenate((policy_term, reward_term), axis=1)
    grouped_feat = features.reshape(N_ROWS, ROW_DEV, D).astype(jnp.float32)
    grouped_terms = both_terms.reshape(N_ROWS, ROW_DEV, 2 * ACTIONS).astype(jnp.float32)
    partial_grad = jnp.einsum("gnd,gna->gda", grouped_feat, grouped_terms, precision=lax.Precision.HIGHEST)
    rounded = lax.optimization_barrier(partial_grad.astype(jnp.bfloat16))
    summed = jnp.sum(rounded.astype(jnp.float32), axis=0)
    return summed[:, :ACTIONS], summed[:, ACTIONS:], row_value
```

```python
import jax
import jax.numpy as jnp
from jax import lax
from jax.sharding import PartitionSpec as P


def on_device(
    features, policy_weight, reward_weight, logged_action, reward_level, logged_propensity
):
    scores = jnp.dot(features, policy_weight, preferred_element_type=jnp.float32)
    predicted = jnp.dot(features, reward_weight, preferred_element_type=jnp.float32)
    act_block = scores.shape[1]
    payoff = reward_level.astype(jnp.float32) * 0.25
    columns = lax.axis_index("acts") * act_block + jnp.arange(act_block, dtype=jnp.int32)
    onehot = logged_action[:, None] == columns[None, :]
    local_max = jnp.max(scores, axis=1)
    exponent = jnp.exp(scores - local_max[:, None])
    zero = jnp.float32(0.0)
    stats = jnp.stack(
        (
            local_max,
            jnp.sum(exponent, axis=1),
            jnp.sum(exponent * predicted, axis=1),
            jnp.sum(jnp.where(onehot, exponent, zero), axis=1),
            jnp.sum(jnp.where(onehot, predicted, zero), axis=1),
        )
    )
    every = lax.all_gather(stats, "acts", axis=0)
    largest = jnp.max(every[:, 0], axis=0)
    rescale = jnp.exp(every[:, 0] - largest)
    row_total = jnp.sum(every[:, 1] * rescale, axis=0)
    mean_pred = jnp.sum(every[:, 2] * rescale, axis=0) / row_total
    picked_exp = jnp.sum(every[:, 3] * rescale, axis=0)
    picked_pred = jnp.sum(every[:, 4], axis=0)
    corrected = picked_exp / row_total / logged_propensity * (payoff - picked_pred)
    row_value = mean_pred + corrected
    probability = exponent * (jnp.exp(local_max - largest) / row_total)[:, None]
    policy_term = (
        probability * (predicted - mean_pred[:, None])
        + corrected[:, None] * (onehot.astype(jnp.float32) - probability)
    ).astype(jnp.bfloat16)
    reward_term = jnp.where(onehot, predicted - payoff[:, None], zero).astype(jnp.bfloat16)

    def grad_of(term):
        partial = lax.dot_general(
            features, term, (((0,), (0,)), ((), ())), preferred_element_type=jnp.float32
        )
        return lax.psum(partial.astype(jnp.bfloat16), "rows").astype(jnp.float32)

    reward_grad = grad_of(reward_term)
    return (grad_of(policy_term), reward_grad, row_value)


def solution(mesh):
    return jax.shard_map(
        on_device,
        mesh=mesh,
        in_specs=(
            P("rows", None),
            P(None, "acts"),
            P(None, "acts"),
            P("rows"),
            P("rows"),
            P("rows"),
        ),
        out_specs=(P(None, "acts"), P(None, "acts"), P("rows")),
        check_vma=False,
    )
```

```python
import functools

import jax
import jax.numpy as jnp
from jax import lax
from jax.experimental import pallas as pl
from jax.experimental.pallas import tpu as pltpu
from jax.sharding import PartitionSpec as P

CORES = 2
F32 = jnp.float32
BF16 = jnp.bfloat16
MESH = pl.DeviceIdType.MESH


def kernel(
    n_rows,
    n_acts,
    dc,
    rc,
    feat_hbm,
    wp_hbm,
    wr_hbm,
    action_ref,
    level_ref,
    prop_ref,
    sums,
    value_ref,
    feat,
    w_raw,
    w_t,
    pred,
    expo,
    term,
    part,
    core_in,
    pair,
    st,
    st_in,
    fin,
    feat_sem,
    w_sem,
    core_send,
    core_recv,
    y_send,
    y_recv,
    own_send,
    own_recv,
    fwd_send,
    fwd_recv,
    loc_sem,
    st_send,
    st_recv,
    fin_send,
    fin_recv,
):
    rows, depth = feat.shape
    acts = pred.shape[0]
    half = acts // CORES
    n_y = n_rows // CORES
    my_row = lax.axis_index("rows")
    my_act = lax.axis_index("acts")
    my_y = my_row // CORES
    my_c = lax.rem(my_row, CORES)
    other_core = {"rows": my_y * CORES + 1 - my_c}
    own_at = pl.multiple_of(my_c * half, half)
    other_at = pl.multiple_of((1 - my_c) * half, half)
    n_d = depth // dc
    n_blocks = rows // rc
    rp = rows // n_acts

    def y_dev(j):
        return {"rows": lax.rem(my_y + j, n_y) * CORES + my_c}

    def act_dev(j):
        return {"acts": lax.rem(my_act + j, n_acts)}

    def feat_copy(b):
        at = pl.ds(pl.multiple_of(b * rc, rc), rc)
        return pltpu.make_async_copy(feat_hbm.at[at], feat.at[at], feat_sem.at[b])

    wr_copy = pltpu.make_async_copy(wr_hbm, w_raw.at[0], w_sem.at[0])
    wp_copy = pltpu.make_async_copy(wp_hbm, w_raw.at[1], w_sem.at[1])
    wr_copy.start()
    for b in range(n_blocks):
        feat_copy(b).start()
        if b == 0:
            wp_copy.start()

    barrier = pltpu.get_barrier_semaphore()
    peers = [other_core] + [y_dev(j) for j in range(1, n_y)] + [act_dev(j) for j in range(1, n_acts)]
    for peer in peers:
        pl.semaphore_signal(barrier, inc=1, device_id=peer, device_id_type=MESH)

    st[...] = jnp.zeros_like(st)

    def transpose_weight(i):
        @pl.loop(0, depth // 256)
        def _(b):
            at = pl.ds(pl.multiple_of(b * 256, 256), 256)
            w_t[i, :, at] = w_raw[i, at, :].T

    def block_at(b):
        return pl.ds(pl.multiple_of(b * rc, rc), rc)

    def times_features(i, at):
        return lax.dot_general(
            w_t[i], feat[at, :], (((1,), (1,)), ((), ())), preferred_element_type=F32
        )

    def chosen(at):
        mine = lax.broadcasted_iota(jnp.int32, (acts, rc), 0) + my_act * acts
        return mine == action_ref[:, at]

    wr_copy.wait()
    transpose_weight(0)

    @pl.loop(0, n_blocks)
    def _(b):
        at = block_at(b)
        feat_copy(b).wait()
        p = times_features(0, at)
        pred[:, at] = p
        onehot = chosen(at)
        payoff = level_ref[:, at].astype(F32) * 0.25
        st[4:5, at] = jnp.sum(jnp.where(onehot, p, 0.0), axis=0, keepdims=True)
        term[:, at] = jnp.where(onehot, p - payoff, 0.0).astype(BF16)

    pl.semaphore_wait(barrier, len(peers))

    def core_copy(k):
        return pltpu.make_async_remote_copy(
            src_ref=part.at[k, pl.ds(other_at, half)],
            dst_ref=core_in.at[k],
            send_sem=core_send.at[k],
            recv_sem=core_recv.at[k],
            device_id=other_core,
            device_id_type=MESH,
        )

    def pair_copy(k, device, send, recv):
        return pltpu.make_async_remote_copy(
            src_ref=pair.at[k],
            dst_ref=sums.at[my_y, k, pl.ds(own_at, half)],
            send_sem=send,
            recv_sem=recv,
            device_id=device,
            device_id_type=MESH,
        )

    def y_copy(k, j):
        return pair_copy(k, y_dev(j), y_send.at[k, j - 1], y_recv.at[k, j - 1])

    def own_copy(k):
        return pair_copy(k, other_core, own_send.at[k], own_recv.at[k])

    def loc_copy(k):
        return pltpu.make_async_copy(
            pair.at[k], sums.at[my_y, k, pl.ds(own_at, half)], loc_sem.at[k]
        )

    def fwd_copy(k, j):
        block = sums.at[lax.rem(my_y + n_y - j, n_y), k, pl.ds(own_at, half)]
        return pltpu.make_async_remote_copy(
            src_ref=block,
            dst_ref=block,
            send_sem=fwd_send.at[k, j - 1],
            recv_sem=fwd_recv.at[k, j - 1],
            device_id=other_core,
            device_id_type=MESH,
        )

    def pass_on(k):
        core_copy(k).wait_recv()
        own = part[k, pl.ds(own_at, half), :].astype(F32)
        pair[k] = (own + core_in[k].astype(F32)).astype(BF16)
        for j in range(1, n_y):
            y_copy(k, j).start()
        own_copy(k).start()
        loc_copy(k).start()

    def chunk(k):
        d_at = pl.ds(pl.multiple_of(lax.rem(k, n_d) * dc, dc), dc)
        part[k] = jnp.dot(term[...], feat[:, d_at], preferred_element_type=F32).astype(BF16)
        core_copy(k).start()

    def chunks(first, last):
        @pl.loop(first, last)
        def _(k):
            chunk(k)

            @pl.when(k > 0)
            def _():
                pass_on(k - 1)

    early = n_d // 4
    middle = (5 * n_d) // 8
    chunks(0, early)

    wp_copy.wait()
    transpose_weight(1)

    @pl.loop(0, n_blocks)
    def _(b):
        at = block_at(b)
        s = times_features(1, at)
        largest = jnp.max(s, axis=0, keepdims=True)
        e = jnp.exp(s - largest)
        expo[:, at] = e
        st[0:1, at] = largest
        st[1:2, at] = jnp.sum(e, axis=0, keepdims=True)
        st[2:3, at] = jnp.sum(e * pred[:, at], axis=0, keepdims=True)
        st[3:4, at] = jnp.sum(jnp.where(chosen(at), e, 0.0), axis=0, keepdims=True)

    def part_at(a):
        return pl.ds(pl.multiple_of(a * rp, rp), rp)

    def st_copy(j):
        return pltpu.make_async_remote_copy(
            src_ref=st.at[:, part_at(lax.rem(my_act + j, n_acts))],
            dst_ref=st_in.at[my_act],
            send_sem=st_send.at[j - 1],
            recv_sem=st_recv.at[j - 1],
            device_id=act_dev(j),
            device_id_type=MESH,
        )

    def fin_copy(j):
        return pltpu.make_async_remote_copy(
            src_ref=fin.at[:, part_at(my_act)],
            dst_ref=fin.at[:, part_at(my_act)],
            send_sem=fin_send.at[j - 1],
            recv_sem=fin_recv.at[j - 1],
            device_id=act_dev(j),
            device_id_type=MESH,
        )

    for j in range(1, n_acts):
        st_copy(j).start()
    st_in[my_act] = st[:, part_at(my_act)]

    chunks(early, middle)

    for j in range(1, n_acts):
        st_copy(j).wait_recv()
    mine = part_at(my_act)
    largest = st_in[0, 0:1, :]
    for a in range(1, n_acts):
        largest = jnp.maximum(largest, st_in[a, 0:1, :])
    row_total = jnp.zeros_like(largest)
    weighted = jnp.zeros_like(largest)
    picked_exp = jnp.zeros_like(largest)
    picked_pred = jnp.zeros_like(largest)
    for a in range(n_acts):
        rescale = jnp.exp(st_in[a, 0:1, :] - largest)
        row_total += st_in[a, 1:2, :] * rescale
        weighted += st_in[a, 2:3, :] * rescale
        picked_exp += st_in[a, 3:4, :] * rescale
        picked_pred += st_in[a, 4:5, :]
    mean_pred = weighted / row_total
    payoff = level_ref[:, mine].astype(F32) * 0.25
    corrected = picked_exp / row_total / prop_ref[:, mine] * (payoff - picked_pred)
    fin[:, mine] = jnp.concatenate(
        (largest, row_total, mean_pred, corrected) + (jnp.zeros_like(largest),) * 4, axis=0
    )
    for j in range(1, n_acts):
        fin_copy(j).start()

    chunks(middle, n_d)

    for j in range(1, n_acts):
        fin_copy(j).wait_recv()

    @pl.loop(0, n_blocks)
    def _(b):
        at = block_at(b)
        mean = fin[2:3, at]
        corr = fin[3:4, at]
        scale = jnp.exp(st[0:1, at] - fin[0:1, at]) / fin[1:2, at]
        probability = expo[:, at] * scale
        onehot = jnp.where(chosen(at), F32(1.0), F32(0.0))
        value_ref[:, at] = mean + corr
        term[:, at] = (
            probability * (pred[:, at] - mean) + corr * (onehot - probability)
        ).astype(BF16)

    chunks(n_d, 2 * n_d)
    pass_on(2 * n_d - 1)

    @pl.loop(0, 2 * n_d)
    def _(k):
        for j in range(1, n_y):
            y_copy(k, j).wait_recv()
            fwd_copy(k, j).start()

    @pl.loop(0, 2 * n_d)
    def _(k):
        core_copy(k).wait_send()
        own_copy(k).wait()
        loc_copy(k).wait()
        for j in range(1, n_y):
            y_copy(k, j).wait_send()
            fwd_copy(k, j).wait()

    for j in range(1, n_acts):
        st_copy(j).wait_send()
        fin_copy(j).wait_send()


def finish(reward_in, policy_in, value_in, policy_out, reward_out, value_out):
    for source, target in ((policy_in, policy_out), (reward_in, reward_out)):
        total = source[0, 0].astype(F32)
        for y in range(1, source.shape[0]):
            total += source[y, 0].astype(F32)
        target[...] = total.T
    value_out[...] = value_in[...]


def on_device(n_rows, n_acts, features, policy_weight, reward_weight, action, level, propensity):
    rows, depth = features.shape
    acts = policy_weight.shape[1]
    half = acts // CORES
    n_y = n_rows // CORES
    dc, rc = 256, 512
    n_d = depth // dc
    rp = rows // n_acts
    dma = pltpu.SemaphoreType.DMA
    others = max(n_y - 1, 1)
    sums, value = pl.pallas_call(
        functools.partial(kernel, n_rows, n_acts, dc, rc),
        out_shape=(
            jax.ShapeDtypeStruct((n_y, 2 * n_d, acts, dc), BF16),
            jax.ShapeDtypeStruct((1, rows), F32),
        ),
        in_specs=[pl.BlockSpec(memory_space=pl.ANY)] * 3
        + [pl.BlockSpec(memory_space=pltpu.VMEM)] * 3,
        out_specs=(
            pl.BlockSpec(memory_space=pl.ANY),
            pl.BlockSpec(memory_space=pltpu.VMEM),
        ),
        scratch_shapes=[
            pltpu.VMEM((rows, depth), BF16),
            pltpu.VMEM((2, depth, acts), BF16),
            pltpu.VMEM((2, acts, depth), BF16),
            pltpu.VMEM((acts, rows), F32),
            pltpu.VMEM((acts, rows), F32),
            pltpu.VMEM((acts, rows), BF16),
            pltpu.VMEM((2 * n_d, acts, dc), BF16),
            pltpu.VMEM((2 * n_d, half, dc), BF16),
            pltpu.VMEM((2 * n_d, half, dc), BF16),
            pltpu.VMEM((8, rows), F32),
            pltpu.VMEM((n_acts, 8, rp), F32),
            pltpu.VMEM((8, rows), F32),
            dma((rows // rc,)),
            dma((2,)),
            dma((2 * n_d,)),
            dma((2 * n_d,)),
            dma((2 * n_d, others)),
            dma((2 * n_d, others)),
            dma((2 * n_d,)),
            dma((2 * n_d,)),
            dma((2 * n_d, others)),
            dma((2 * n_d, others)),
            dma((2 * n_d,)),
            dma((n_acts - 1,)),
            dma((n_acts - 1,)),
            dma((n_acts - 1,)),
            dma((n_acts - 1,)),
        ],
        compiler_params=pltpu.CompilerParams(
            collective_id=0, has_side_effects=True, vmem_limit_bytes=62 * 1024 * 1024
        ),
        cost_estimate=pl.CostEstimate(
            flops=8 * rows * depth * acts,
            bytes_accessed=2 * rows * depth + 16 * depth * acts,
            transcendentals=rows * acts,
        ),
    )(
        features,
        policy_weight,
        reward_weight,
        action.reshape(1, rows),
        level.reshape(1, rows),
        propensity.reshape(1, rows),
    )
    grad_spec = pl.BlockSpec((dc, acts), lambda i: (i, 0))
    policy_grad, reward_grad, row_value = pl.pallas_call(
        finish,
        grid=(n_d,),
        out_shape=(
            jax.ShapeDtypeStruct((depth, acts), F32),
            jax.ShapeDtypeStruct((depth, acts), F32),
            jax.ShapeDtypeStruct((1, rows), F32),
        ),
        in_specs=[
            pl.BlockSpec((n_y, 1, acts, dc), lambda i: (0, i, 0, 0)),
            pl.BlockSpec((n_y, 1, acts, dc), lambda i: (0, i + n_d, 0, 0)),
            pl.BlockSpec((1, rows), lambda i: (0, 0)),
        ],
        out_specs=(grad_spec, grad_spec, pl.BlockSpec((1, rows), lambda i: (0, 0))),
        compiler_params=pltpu.CompilerParams(vmem_limit_bytes=32 * 1024 * 1024),
    )(sums, sums, value)
    return policy_grad, reward_grad, row_value.reshape(rows)


def solution(mesh):
    return jax.shard_map(
        functools.partial(on_device, mesh.shape["rows"], mesh.shape["acts"]),
        mesh=mesh,
        in_specs=(
            P("rows", None),
            P(None, "acts"),
            P(None, "acts"),
            P("rows"),
            P("rows"),
            P("rows"),
        ),
        out_specs=(P(None, "acts"), P(None, "acts"), P("rows")),
        check_vma=False,
    )
```

```python
import functools

import jax
import jax.numpy as jnp
from jax import lax
from jax.experimental import pallas as pl
from jax.experimental.pallas import tpu as pltpu
from jax.sharding import PartitionSpec as P

CORES = 2
F32 = jnp.float32
BF16 = jnp.bfloat16
MESH = pl.DeviceIdType.MESH


def kernel(
    n_rows,
    n_acts,
    dc,
    rc,
    feat_hbm,
    wp_hbm,
    wr_hbm,
    action_ref,
    level_ref,
    prop_ref,
    sums,
    value_ref,
    feat,
    w_raw,
    w_t,
    pred,
    expo,
    term,
    late_term,
    part,
    core_in,
    pair,
    st,
    st_in,
    fin,
    feat_sem,
    w_sem,
    core_send,
    core_recv,
    y_send,
    y_recv,
    own_send,
    own_recv,
    fwd_send,
    fwd_recv,
    loc_sem,
    st_send,
    st_recv,
    fin_send,
    fin_recv,
):
    rows, depth = feat.shape
    acts = pred.shape[0]
    half = acts // CORES
    n_y = n_rows // CORES
    my_row = lax.axis_index("rows")
    my_act = lax.axis_index("acts")
    my_y = my_row // CORES
    my_c = lax.rem(my_row, CORES)
    other_core = {"rows": my_y * CORES + 1 - my_c}
    own_at = pl.multiple_of(my_c * half, half)
    other_at = pl.multiple_of((1 - my_c) * half, half)
    n_d = depth // dc
    n_blocks = rows // rc
    rp = rows // n_acts

    def y_dev(j):
        return {"rows": lax.rem(my_y + j, n_y) * CORES + my_c}

    def act_dev(j):
        return {"acts": lax.rem(my_act + j, n_acts)}

    def feat_copy(b):
        at = pl.ds(pl.multiple_of(b * rc, rc), rc)
        return pltpu.make_async_copy(feat_hbm.at[at], feat.at[at], feat_sem.at[b])

    wr_copy = pltpu.make_async_copy(wr_hbm, w_raw, w_sem.at[0])
    wp_copy = pltpu.make_async_copy(wp_hbm, w_raw, w_sem.at[1])
    wr_copy.start()
    for b in range(n_blocks):
        feat_copy(b).start()

    barrier = pltpu.get_barrier_semaphore()
    peers = [other_core] + [y_dev(j) for j in range(1, n_y)] + [act_dev(j) for j in range(1, n_acts)]
    for peer in peers:
        pl.semaphore_signal(barrier, inc=1, device_id=peer, device_id_type=MESH)

    st[...] = jnp.zeros_like(st)

    def transpose_weight(i):
        @pl.loop(0, depth // 256)
        def _(b):
            at = pl.ds(pl.multiple_of(b * 256, 256), 256)
            w_t[i, :, at] = w_raw[at, :].T

    def block_at(b):
        return pl.ds(pl.multiple_of(b * rc, rc), rc)

    def times_features(i, at):
        return lax.dot_general(
            w_t[i], feat[at, :], (((1,), (1,)), ((), ())), preferred_element_type=F32
        )

    def chosen(at):
        mine = lax.broadcasted_iota(jnp.int32, (acts, rc), 0) + my_act * acts
        return mine == action_ref[:, at]

    wr_copy.wait()
    transpose_weight(0)
    wp_copy.start()

    def predict(b):
        at = block_at(b)
        pred[:, at] = times_features(0, at)

    def reward_terms(b):
        at = block_at(b)
        p = pred[:, at]
        onehot = chosen(at)
        payoff = level_ref[:, at].astype(F32) * 0.25
        st[4:5, at] = jnp.sum(jnp.where(onehot, p, 0.0), axis=0, keepdims=True)
        term[:, at] = jnp.where(onehot, p - payoff, 0.0).astype(BF16)

    feat_copy(0).wait()
    predict(0)

    @pl.loop(1, n_blocks)
    def _(b):
        feat_copy(b).wait()
        reward_terms(b - 1)
        predict(b)

    reward_terms(n_blocks - 1)

    pl.semaphore_wait(barrier, len(peers))

    def core_copy(k):
        return pltpu.make_async_remote_copy(
            src_ref=part.at[k, pl.ds(other_at, half)],
            dst_ref=core_in.at[k],
            send_sem=core_send.at[k],
            recv_sem=core_recv.at[k],
            device_id=other_core,
            device_id_type=MESH,
        )

    def pair_copy(k, device, send, recv):
        return pltpu.make_async_remote_copy(
            src_ref=pair.at[k],
            dst_ref=sums.at[my_y, k, pl.ds(own_at, half)],
            send_sem=send,
            recv_sem=recv,
            device_id=device,
            device_id_type=MESH,
        )

    def y_copy(k, j):
        return pair_copy(k, y_dev(j), y_send.at[k, j - 1], y_recv.at[k, j - 1])

    def own_copy(k):
        return pair_copy(k, other_core, own_send.at[k], own_recv.at[k])

    def loc_copy(k):
        return pltpu.make_async_copy(
            pair.at[k], sums.at[my_y, k, pl.ds(own_at, half)], loc_sem.at[k]
        )

    def fwd_copy(k, j):
        block = sums.at[lax.rem(my_y + n_y - j, n_y), k, pl.ds(own_at, half)]
        return pltpu.make_async_remote_copy(
            src_ref=block,
            dst_ref=block,
            send_sem=fwd_send.at[k, j - 1],
            recv_sem=fwd_recv.at[k, j - 1],
            device_id=other_core,
            device_id_type=MESH,
        )

    def pass_on(k):
        core_copy(k).wait_recv()
        own = part[k, pl.ds(own_at, half), :].astype(F32)
        pair[k] = (own + core_in[k].astype(F32)).astype(BF16)
        for j in range(1, n_y):
            y_copy(k, j).start()
        own_copy(k).start()
        loc_copy(k).start()

    def chunk(k, source):
        d_at = pl.ds(pl.multiple_of(lax.rem(k, n_d) * dc, dc), dc)
        part[k] = jnp.dot(source[...], feat[:, d_at], preferred_element_type=F32).astype(BF16)
        core_copy(k).start()

    def chunks(first, last, source, beside=None):
        @pl.loop(first, last)
        def _(k):
            if beside is not None:
                beside(k - first)
            chunk(k, source)

            @pl.when(k > 0)
            def _():
                pass_on(k - 1)

    early = n_d // 4
    middle = n_d // 2
    late = (3 * n_d) // 4
    chunks(0, early, term)

    wp_copy.wait()
    transpose_weight(1)

    def score(b):
        at = block_at(b)
        expo[:, at] = times_features(1, at)

    def exponents(b):
        at = block_at(b)
        s = expo[:, at]
        largest = jnp.max(s, axis=0, keepdims=True)
        e = jnp.exp(s - largest)
        expo[:, at] = e
        st[0:1, at] = largest
        st[1:2, at] = jnp.sum(e, axis=0, keepdims=True)
        st[2:3, at] = jnp.sum(e * pred[:, at], axis=0, keepdims=True)
        st[3:4, at] = jnp.sum(jnp.where(chosen(at), e, 0.0), axis=0, keepdims=True)

    score(0)

    @pl.loop(1, n_blocks)
    def _(b):
        exponents(b - 1)
        score(b)

    exponents(n_blocks - 1)

    def part_at(a):
        return pl.ds(pl.multiple_of(a * rp, rp), rp)

    def st_copy(j):
        return pltpu.make_async_remote_copy(
            src_ref=st.at[:, part_at(lax.rem(my_act + j, n_acts))],
            dst_ref=st_in.at[my_act],
            send_sem=st_send.at[j - 1],
            recv_sem=st_recv.at[j - 1],
            device_id=act_dev(j),
            device_id_type=MESH,
        )

    def fin_copy(j):
        return pltpu.make_async_remote_copy(
            src_ref=fin.at[:, part_at(my_act)],
            dst_ref=fin.at[:, part_at(my_act)],
            send_sem=fin_send.at[j - 1],
            recv_sem=fin_recv.at[j - 1],
            device_id=act_dev(j),
            device_id_type=MESH,
        )

    for j in range(1, n_acts):
        st_copy(j).start()
    st_in[my_act] = st[:, part_at(my_act)]

    chunks(early, middle, term)

    for j in range(1, n_acts):
        st_copy(j).wait_recv()
    mine = part_at(my_act)
    largest = st_in[0, 0:1, :]
    for a in range(1, n_acts):
        largest = jnp.maximum(largest, st_in[a, 0:1, :])
    row_total = jnp.zeros_like(largest)
    weighted = jnp.zeros_like(largest)
    picked_exp = jnp.zeros_like(largest)
    picked_pred = jnp.zeros_like(largest)
    for a in range(n_acts):
        rescale = jnp.exp(st_in[a, 0:1, :] - largest)
        row_total += st_in[a, 1:2, :] * rescale
        weighted += st_in[a, 2:3, :] * rescale
        picked_exp += st_in[a, 3:4, :] * rescale
        picked_pred += st_in[a, 4:5, :]
    mean_pred = weighted / row_total
    payoff = level_ref[:, mine].astype(F32) * 0.25
    corrected = picked_exp / row_total / prop_ref[:, mine] * (payoff - picked_pred)
    fin[:, mine] = jnp.concatenate(
        (largest, row_total, mean_pred, corrected) + (jnp.zeros_like(largest),) * 4, axis=0
    )
    for j in range(1, n_acts):
        fin_copy(j).start()

    chunks(middle, late, term)

    for j in range(1, n_acts):
        fin_copy(j).wait_recv()

    def policy_terms(b):
        at = block_at(b)
        mean = fin[2:3, at]
        corr = fin[3:4, at]
        scale = jnp.exp(st[0:1, at] - fin[0:1, at]) / fin[1:2, at]
        probability = expo[:, at] * scale
        onehot = jnp.where(chosen(at), F32(1.0), F32(0.0))
        value_ref[:, at] = mean + corr
        late_term[:, at] = (
            probability * (pred[:, at] - mean) + corr * (onehot - probability)
        ).astype(BF16)

    share = n_blocks // (n_d - late)

    def policy_share(i):
        for b in range(share):
            policy_terms(i * share + b)

    chunks(late, n_d, term, policy_share)
    chunks(n_d, 2 * n_d, late_term)
    pass_on(2 * n_d - 1)

    @pl.loop(0, 2 * n_d)
    def _(k):
        for j in range(1, n_y):
            y_copy(k, j).wait_recv()
            fwd_copy(k, j).start()

    @pl.loop(0, 2 * n_d)
    def _(k):
        core_copy(k).wait_send()
        own_copy(k).wait()
        loc_copy(k).wait()
        for j in range(1, n_y):
            y_copy(k, j).wait_send()
            fwd_copy(k, j).wait()

    for j in range(1, n_acts):
        st_copy(j).wait_send()
        fin_copy(j).wait_send()


def finish(reward_in, policy_in, value_in, policy_out, reward_out, value_out):
    for source, target in ((policy_in, policy_out), (reward_in, reward_out)):
        total = source[0, 0].astype(F32)
        for y in range(1, source.shape[0]):
            total += source[y, 0].astype(F32)
        target[...] = total.T
    value_out[...] = value_in[...]


def on_device(n_rows, n_acts, features, policy_weight, reward_weight, action, level, propensity):
    rows, depth = features.shape
    acts = policy_weight.shape[1]
    half = acts // CORES
    n_y = n_rows // CORES
    dc, rc = 256, 512
    n_d = depth // dc
    rp = rows // n_acts
    dma = pltpu.SemaphoreType.DMA
    others = max(n_y - 1, 1)
    sums, value = pl.pallas_call(
        functools.partial(kernel, n_rows, n_acts, dc, rc),
        out_shape=(
            jax.ShapeDtypeStruct((n_y, 2 * n_d, acts, dc), BF16),
            jax.ShapeDtypeStruct((1, rows), F32),
        ),
        in_specs=[pl.BlockSpec(memory_space=pl.ANY)] * 3
        + [pl.BlockSpec(memory_space=pltpu.VMEM)] * 3,
        out_specs=(
            pl.BlockSpec(memory_space=pl.ANY),
            pl.BlockSpec(memory_space=pltpu.VMEM),
        ),
        scratch_shapes=[
            pltpu.VMEM((rows, depth), BF16),
            pltpu.VMEM((depth, acts), BF16),
            pltpu.VMEM((2, acts, depth), BF16),
            pltpu.VMEM((acts, rows), F32),
            pltpu.VMEM((acts, rows), F32),
            pltpu.VMEM((acts, rows), BF16),
            pltpu.VMEM((acts, rows), BF16),
            pltpu.VMEM((2 * n_d, acts, dc), BF16),
            pltpu.VMEM((2 * n_d, half, dc), BF16),
            pltpu.VMEM((2 * n_d, half, dc), BF16),
            pltpu.VMEM((8, rows), F32),
            pltpu.VMEM((n_acts, 8, rp), F32),
            pltpu.VMEM((8, rows), F32),
            dma((rows // rc,)),
            dma((2,)),
            dma((2 * n_d,)),
            dma((2 * n_d,)),
            dma((2 * n_d, others)),
            dma((2 * n_d, others)),
            dma((2 * n_d,)),
            dma((2 * n_d,)),
            dma((2 * n_d, others)),
            dma((2 * n_d, others)),
            dma((2 * n_d,)),
            dma((n_acts - 1,)),
            dma((n_acts - 1,)),
            dma((n_acts - 1,)),
            dma((n_acts - 1,)),
        ],
        compiler_params=pltpu.CompilerParams(
            collective_id=0, has_side_effects=True, vmem_limit_bytes=62 * 1024 * 1024
        ),
        cost_estimate=pl.CostEstimate(
            flops=8 * rows * depth * acts,
            bytes_accessed=2 * rows * depth + 16 * depth * acts,
            transcendentals=rows * acts,
        ),
    )(
        features,
        policy_weight,
        reward_weight,
        action.reshape(1, rows),
        level.reshape(1, rows),
        propensity.reshape(1, rows),
    )
    grad_spec = pl.BlockSpec((dc, acts), lambda i: (i, 0))
    policy_grad, reward_grad, row_value = pl.pallas_call(
        finish,
        grid=(n_d,),
        out_shape=(
            jax.ShapeDtypeStruct((depth, acts), F32),
            jax.ShapeDtypeStruct((depth, acts), F32),
            jax.ShapeDtypeStruct((1, rows), F32),
        ),
        in_specs=[
            pl.BlockSpec((n_y, 1, acts, dc), lambda i: (0, i, 0, 0)),
            pl.BlockSpec((n_y, 1, acts, dc), lambda i: (0, i + n_d, 0, 0)),
            pl.BlockSpec((1, rows), lambda i: (0, 0)),
        ],
        out_specs=(grad_spec, grad_spec, pl.BlockSpec((1, rows), lambda i: (0, 0))),
        compiler_params=pltpu.CompilerParams(vmem_limit_bytes=62 * 1024 * 1024),
    )(sums, sums, value)
    return policy_grad, reward_grad, row_value.reshape(rows)


def solution(mesh):
    return jax.shard_map(
        functools.partial(on_device, mesh.shape["rows"], mesh.shape["acts"]),
        mesh=mesh,
        in_specs=(
            P("rows", None),
            P(None, "acts"),
            P(None, "acts"),
            P("rows"),
            P("rows"),
            P("rows"),
        ),
        out_specs=(P(None, "acts"), P(None, "acts"), P("rows")),
        check_vma=False,
    )
```
